256 devices in a mesh: dp: 8 (over z), expert: 16 (over x, y), opt: 2 (over core).
Axes of the slice: x: 4, y: 4, z: 8, core: 2. Of those that a mesh axis runs over, the one named last changes fastest.
Arguments:
- tokens: bfloat16 [65536, 4096], P(('dp', 'expert', 'opt')), may hold values from -6 to 6
- routing: int32 [65536, 8], P(('dp', 'expert', 'opt')), may hold values from 0 to 127, all different within a row; in each aligned block of 256 rows (0 to 255, 256 to 511, ...) at most 32 rows name the same one
- grad_gate: bfloat16 [8, 16, 2, 512, 1536], P('dp', 'expert', 'opt'), may hold values from -0.0625 to 0.0625
- touched_mask: int32 [16, 32, 12], P('expert', ('dp', 'opt')), may hold values 0 or 1
- params: float32 [16, 4096, 1536], P('expert', ('dp', 'opt')), may hold values from -3 to 3
- moment_one: float32 [16, 4096, 1536], P('expert', ('dp', 'opt')), may hold values from -2 to 2
- moment_two: float32 [16, 4096, 1536], P('expert', ('dp', 'opt')), may hold values from 0.01 to 1
Outputs:
- new_params: float32 [16, 4096, 1536], P('expert', ('dp', 'opt'))
- new_moment_one: float32 [16, 4096, 1536], P('expert', ('dp', 'opt'))
- new_moment_two: float32 [16, 4096, 1536], P('expert', ('dp', 'opt'))
The draws below stay inside these ranges and needn't reach their ends.
Inputs may be any that keep to these rules, and one draw needn't show every extreme that they name: `routing`: among the 2048 entries of one device no expert is named more than 32 times, a bound that some block reaches; a token's 8 experts differ.
All inputs are finite; a program needn't handle non-finite values. No bound on the sum of `touched_mask` on one device may be relied on, other than what follows from the above.
Results may differ from the reference program's by a relative error of at most 0.0006.
Values may be sent and summed in bfloat16 or wider, within the bound.
No kernel may reach another device: no remote copies, remote signals or barrier semaphores. Data moves between devices by JAX's collectives and lax.ppermute only.
A program may use at most 128 MiB of HBM per device.

```python
import math
import jax
import jax.numpy as jnp
import numpy as np
from jax import lax

D = 4096
FF = 1536
EXPERTS_ALL = 128
TOP = 8
TOK_DEV = 256
CAP = 32
TILE = 128
EXPERTS = 16
TOKENS = 65536
SLOTS = 512
N_DP = 8
N_EXPERT = 16
N_OPT = 2


def set_ends(drawn, key, smallest, largest):
    longest = drawn.shape.index(max(drawn.shape))
    spots = []
    for shift in (0, 1):
        where = [jax.random.randint(jax.random.fold_in(key, axis), (), 0, length) for axis, length in enumerate(drawn.shape)]
        where[longest] = (where[longest] + shift) % drawn.shape[longest]
        spots.append(tuple(where))
    return drawn.at[spots[0]].set(smallest).at[spots[1]].set(largest)


def shard_levels(key, dims, pieces, least, largest):
    factor_of, own = 1.0, jax.random.fold_in(key, 6)
    for position, parts in pieces:
        draws = jnp.exp(jax.random.uniform(jax.random.fold_in(own, position), (parts,), jnp.float32, least / len(pieces), largest / len(pieces)))
        factor_of = factor_of * jnp.repeat(draws, dims[position] // parts).reshape([-1 if axis == position else 1 for axis in range(len(dims))])
    return factor_of


def assign_block(rng, own, number, rows, amount, top, reach, skew):
    ranking = jax.random.permutation(rng, amount)
    crowded, usual = shares(amount, rows * top, reach, skew, True), shares(amount, rows * top, reach, skew, False)
    places = jnp.arange(amount)

    def named(tallies, rotation):
        used = int((tallies > 0).sum())
        fixed = max(1, used // 4)
        shifted = fixed + (places - fixed + rotation * (used - fixed)) % max(1, amount - fixed)
        return jnp.zeros((amount,), jnp.int32).at[ranking[jnp.where(places < fixed, places, shifted)]].set(jnp.asarray(tallies, jnp.int32))

    tallies = jnp.where(number % 4 == 0, named(crowded, number // 4), named(usual, number - number // 4 - 1))
    mixed = jax.random.permutation(jax.random.fold_in(own, 3), amount)
    giver, receiver = mixed[0:amount // 2 * 2:2], mixed[1:amount // 2 * 2:2]
    room = jnp.minimum(tallies[giver] - 1, reach - tallies[receiver]) // 2
    room = jnp.where((giver == ranking[0]) | (receiver == ranking[0]) | (tallies[receiver] == 0), 0, jnp.maximum(room, 0))
    shifted = jax.random.randint(jax.random.fold_in(own, 4), (amount // 2,), 0, 1 << 20) % (room + 1)
    tallies = tallies.at[giver].add(-shifted).at[receiver].add(shifted)
    labels = jnp.searchsorted(jnp.cumsum(tallies), jnp.arange(rows * top), side="right").astype(jnp.int32)
    table = labels.reshape(top, rows).T
    table = table[jax.random.permutation(jax.random.fold_in(own, 1), rows)]
    rotation = jax.random.randint(jax.random.fold_in(own, 2), (rows, 1), 0, top)
    return jnp.take_along_axis(table, (jnp.arange(top)[None, :] + rotation) % top, axis=1)


def shares(number_of, total, bound, lean, full):
    weights = [(1 << 20) // math.isqrt(standing ** lean) + 1 for standing in range(1, number_of + 1)]
    largest = bound if full else min(bound, max(-(-total // number_of), total * weights[0] // sum(weights)))
    least = 1 if total - largest >= number_of - 1 else 0
    holding, spare = [largest] + [least] * (number_of - 1), total - largest - least * (number_of - 1)
    while spare > 0:
        movable = [i for i in range(1, number_of) if holding[i] < largest] or [i for i in range(1, number_of) if holding[i] < bound]
        pool, left = sum([weights[i] for i in movable]), spare
        for i in movable:
            addition = min(bound - holding[i], max(1, left * weights[i] // pool), spare)
            holding[i] = holding[i] + addition
            spare = spare - addition
    return np.array(holding)


def gaussian(own_key, extent, spread, limit, split=(), kind=jnp.bfloat16):
    values = spread * jax.random.normal(own_key, extent, jnp.float32)
    if split:
        values = values * shard_levels(own_key, extent, split, -0.22, 0.18)
    return jnp.clip(values, -limit, limit).astype(kind)


def setup_inputs(seed: int = 0) -> dict:
    key_of = jax.random.split(jax.random.key(seed), 8)
    tokens = gaussian(key_of[0], (TOKENS, D), 1.0, 6.0, ((0, 256),))
    routing_keys = jax.random.split(jax.random.fold_in(key_of[1], 1), TOKENS // TOK_DEV)
    routing_turns = jax.random.permutation(jax.random.fold_in(key_of[1], 3), TOKENS // TOK_DEV)
    routing = jax.vmap(lambda own, number: assign_block(jax.random.fold_in(key_of[1], 2), own, number, TOK_DEV, EXPERTS_ALL, TOP, CAP, 2))(routing_keys, routing_turns).reshape((TOKENS, TOP))
    grad_gate = gaussian(key_of[2], (N_DP, EXPERTS, N_OPT, SLOTS, FF), (N_DP * N_OPT * SLOTS) ** -0.5, 0.0625, ((0, 8), (1, 16), (2, 2)))
    touched_mask = set_ends((jax.random.randint(key_of[3], (EXPERTS, D // TILE, FF // TILE), 0, 4) < 3).astype(jnp.int32), jax.random.fold_in(key_of[3], 1), 0, 1)
    params = gaussian(key_of[4], (EXPERTS, D, FF), 0.5, 3.0, ((0, 16), (1, 16)), jnp.float32)
    moment_one = gaussian(key_of[5], (EXPERTS, D, FF), 0.3, 2.0, ((0, 16), (1, 16)), jnp.float32)
    moment_two = jnp.clip(jnp.exp(math.log(1.0) - 4.6051702 * jax.random.uniform(key_of[6], (EXPERTS, D, FF), jnp.float32) ** shard_levels(key_of[6], (EXPERTS, D, FF), ((0, 16), (1, 16)), -0.2, 0.2)), 0.01, 1.0)
    return dict(tokens=tokens, routing=routing, grad_gate=grad_gate, touched_mask=touched_mask, params=params, moment_one=moment_one, moment_two=moment_two)


def slots_of(flat_routes):
    onehot = (flat_routes[..., :, None] == jnp.arange(EXPERTS, dtype=jnp.int32)).astype(jnp.int32)
    before = jnp.cumsum(onehot, axis=-2) - onehot
    return lax.optimization_barrier(jnp.sum(before * onehot, axis=-1)).astype(jnp.int32)

def expand_tiles(tiles):
    return jnp.repeat(jnp.repeat(tiles, TILE, axis=0), TILE, axis=1)

def reference(tokens, routing, grad_gate, touched_mask, params, moment_one, moment_two):
    shaped = tokens.reshape(N_DP, N_EXPERT, N_OPT, TOK_DEV, D)
    routes = routing.reshape(N_DP, N_EXPERT, N_OPT, TOK_DEV * TOP)
    slots = slots_of(routes).reshape(N_DP, N_EXPERT, N_OPT, TOK_DEV, TOP)
    routes = routes.reshape(N_DP, N_EXPERT, N_OPT, TOK_DEV, TOP)
    grid = (N_DP, N_EXPERT, N_OPT, TOK_DEV)
    r_idx = lax.broadcasted_iota(jnp.int32, grid, 0)
    s_idx = lax.broadcasted_iota(jnp.int32, grid, 1)
    o_idx = lax.broadcasted_iota(jnp.int32, grid, 2)
    grads_by_expert = jnp.transpose(grad_gate, (1, 0, 2, 3, 4))

    def one_expert(inputs):
        expert_id, dg_all, mask_tiles, weight, first, second = inputs
        gathered = jnp.zeros((N_DP, N_OPT, N_EXPERT, CAP, D), jnp.bfloat16)
        for k in range(TOP):
            slot_k = jnp.where(routes[..., k] == expert_id, slots[..., k], CAP).astype(jnp.int32)
            gathered = gathered.at[r_idx, o_idx, s_idx, slot_k].set(shaped, mode='drop')
        gathered = gathered.reshape(N_DP, N_OPT, SLOTS, D)

        def add_group(total, index):
            r = index // N_OPT
            o = index % N_OPT
            part = jnp.dot(gathered[r, o].T, dg_all[r, o], preferred_element_type=jnp.float32)
            part = lax.optimization_barrier(part.astype(jnp.bfloat16)).astype(jnp.float32)
            return (total + part, None)
        grad, _ = lax.scan(add_group, jnp.zeros((D, FF), jnp.float32), jnp.arange(N_DP * N_OPT, dtype=jnp.int32))
        live = expand_tiles(mask_tiles) > 0
        first_new = 0.9 * first + 0.1 * grad
        second_new = 0.95 * second + 0.05 * grad * grad
        step = first_new / (1.0 - 0.9 ** 10) / (jnp.sqrt(second_new / (1.0 - 0.95 ** 10)) + 1e-08)
        weight_new = weight - 0.01 * (step + 0.1 * weight)
        return (jnp.where(live, weight_new, weight), jnp.where(live, first_new, first), jnp.where(live, second_new, second))
    expert_ids = jnp.arange(EXPERTS, dtype=jnp.int32)
    new_params, new_one, new_two = lax.map(one_expert, (expert_ids, grads_by_expert, touched_mask, params, moment_one, moment_two))
    return (new_params, new_one, new_two)
```

```python
import jax
import jax.numpy as jnp
from jax import lax
from jax.experimental import pallas as pl
from jax.experimental.pallas import tpu as pltpu
from jax.sharding import PartitionSpec as P

TILE = 128
CAP = 32
EXPERTS = 16
N_DP = 8
HALF = 256
WIRE_SCALE = 16.0


def dispatch_kernel(blocks_ref, routes_ref, *refs):
    *token_refs, out_ref, pick_ref = refs
    count = token_refs[0].shape[0]

    @pl.when(pl.program_id(0) == 0)
    def _():
        expert = lax.broadcasted_iota(jnp.int32, (EXPERTS, count), 0)
        named = routes_ref[0:1, :] == expert
        for k in range(1, routes_ref.shape[0]):
            named = jnp.logical_or(named, routes_ref[k : k + 1, :] == expert)
        named = named.astype(jnp.float32)
        row = lax.broadcasted_iota(jnp.int32, (count, count), 0)
        column = lax.broadcasted_iota(jnp.int32, (count, count), 1)
        earlier = (row < column).astype(jnp.bfloat16)
        before = jnp.dot(named.astype(jnp.bfloat16), earlier, preferred_element_type=jnp.float32)
        place = jnp.where(named > 0, before, -1.0).astype(jnp.int32)
        slot = lax.broadcasted_iota(jnp.int32, (CAP, count), 0)
        for e in range(EXPERTS):
            hit = place[e : e + 1, :] == slot
            pick_ref[e * CAP : (e + 1) * CAP, :] = hit.astype(jnp.float32).astype(jnp.bfloat16)

    for j, token_ref in enumerate(token_refs):
        out_ref[:, j * HALF : (j + 1) * HALF] = jnp.dot(
            pick_ref[...], token_ref[...], preferred_element_type=jnp.float32
        ).astype(out_ref.dtype)


def dispatch(blocks, routes, tokens):
    rows = EXPERTS * CAP
    count = tokens.shape[0]
    halves = blocks.shape[0] // 2

    def block(j):
        return pl.BlockSpec((count, HALF), lambda i, blocks: (0, blocks[i * halves + j]))

    return pl.pallas_call(
        dispatch_kernel,
        grid_spec=pltpu.PrefetchScalarGridSpec(
            num_scalar_prefetch=1,
            grid=(2,),
            in_specs=[pl.BlockSpec(routes.shape, lambda i, blocks: (0, 0))]
            + [block(j) for j in range(halves)],
            out_specs=pl.BlockSpec((rows, halves * HALF), lambda i, blocks: (i, 0)),
            scratch_shapes=[pltpu.VMEM((rows, count), jnp.bfloat16)],
        ),
        out_shape=jax.ShapeDtypeStruct((2 * rows, halves * HALF), jnp.bfloat16),
        compiler_params=pltpu.CompilerParams(vmem_limit_bytes=60 << 20),
        cost_estimate=pl.CostEstimate(
            flops=2 * 2 * rows * halves * HALF * count,
            bytes_accessed=2 * halves * HALF * (count + rows) * 2,
            transcendentals=0,
        ),
        name="dispatch",
    )(blocks, routes, *([tokens] * halves))


def product_kernel(core_ref, *refs):
    *x_refs, g_mine, g_other, out_ref = refs
    count = len(x_refs) // 2

    def part(x, g):
        contract = (((0,), (0,)), ((), ()))
        p = lax.dot_general(x, g, contract, preferred_element_type=jnp.float32)
        return p.astype(jnp.bfloat16).astype(jnp.float32)

    for j in range(count):
        out_ref[j * HALF : (j + 1) * HALF, :] = (
            part(x_refs[j][0], g_mine[...]) + part(x_refs[count + j][0], g_other[...])
        ) * WIRE_SCALE


def product(core, arrived, mine, other, blocks):
    slots, hidden = mine.shape
    tile = 768
    rows = len(blocks) * HALF

    def of_mine(j):
        return pl.BlockSpec((1, slots, HALF), lambda n, core: (core[0], 0, j))

    def of_other(j):
        return pl.BlockSpec((1, slots, HALF), lambda n, core: (1 - core[0], 0, j))

    return pl.pallas_call(
        product_kernel,
        grid_spec=pltpu.PrefetchScalarGridSpec(
            num_scalar_prefetch=1,
            grid=(hidden // tile,),
            in_specs=[of_mine(j) for j in blocks]
            + [of_other(j) for j in blocks]
            + [
                pl.BlockSpec((slots, tile), lambda n, core: (0, n)),
                pl.BlockSpec((slots, tile), lambda n, core: (0, n)),
            ],
            out_specs=pl.BlockSpec((rows, tile), lambda n, core: (0, n)),
        ),
        out_shape=jax.ShapeDtypeStruct((rows, hidden), jnp.float32),
        compiler_params=pltpu.CompilerParams(vmem_limit_bytes=24 << 20),
        cost_estimate=pl.CostEstimate(
            flops=2 * 2 * slots * rows * hidden,
            bytes_accessed=4 * slots * (rows + hidden) + 4 * rows * hidden,
            transcendentals=0,
        ),
        name="product",
    )(core, *([arrived] * (2 * len(blocks))), mine, other)


def after(x, *others):
    return lax.optimization_barrier((x,) + others)[0]


def per_device(tokens, routing, grad_gate, touched_mask, params, moment_one, moment_two):
    r = lax.axis_index("dp")
    core = lax.axis_index("opt").astype(jnp.int32).reshape(1)
    slots = EXPERTS * CAP
    routes = routing.T
    mine = grad_gate[0, 0, 0]
    other = lax.ppermute(mine, "opt", [(0, 1), (1, 0)])

    ahead = [(i * 2 + o, ((i + (1 - 2 * o)) % N_DP) * 2 + o) for i in range(N_DP) for o in range(2)]
    across = [(i * 2 + o, ((i + (1 - 2 * o)) % N_DP) * 2 + 1 - o) for i in range(N_DP) for o in range(2)]

    def gathered(pairs):
        up = [2 * ((r + k) % N_DP) + other_core for k, other_core in pairs]
        down = [2 * ((r - k) % N_DP) + 1 - other_core for k, other_core in pairs]
        return dispatch(jnp.stack(up + down).astype(jnp.int32), routes, tokens)

    def exchange(sent):
        sent = sent.reshape(2 * EXPERTS, CAP, -1)
        return lax.all_to_all(sent, ("opt", "expert"), 0, 0, tiled=True).reshape(2, slots, -1)

    def totals(arrived, blocks):
        out = product(core, arrived, mine, other, blocks)
        return [out[j * HALF : (j + 1) * HALF] for j in range(len(blocks))]

    def plus(x, received):
        return x + received.astype(jnp.float32)

    def pack(x):
        return x.astype(jnp.float16)

    def shift(x, pairs):
        return lax.ppermute(x, ("dp", "opt"), pairs)

    sent = gathered([(4, 0), (3, 1), (3, 0), (2, 1)])
    arrived = exchange(sent)
    sent = after(gathered([(2, 0), (1, 1), (1, 0), (0, 0)]), sent)
    arrived, sent = lax.optimization_barrier((arrived, sent))
    (own,) = totals(arrived, [0])
    near_out = pack(own)
    near = shift(near_out, ahead)
    late = exchange(after(sent, near_out))
    three_b, three_a, two_b = totals(after(arrived, near_out), [1, 2, 3])
    far_out = pack(three_b)
    far = shift(far_out, ahead)
    near_out = pack(plus(three_a, after(near, far_out)))
    near = shift(near_out, ahead)
    far_out = pack(plus(two_b, after(far, near_out)))
    far = shift(far_out, ahead)
    (two_a,) = totals(late, [0])
    near_out = pack(plus(two_a, after(near, far_out)))
    near = shift(near_out, ahead)
    one_b, one_a, own = totals(after(late, near_out), [1, 2, 3])
    far_out = pack(plus(one_b, after(far, near_out)))
    far = shift(far_out, across)
    near_out = pack(plus(one_a, after(near, far_out)))
    near = shift(near_out, ahead)
    grad = plus(plus(own, far), near) * (1.0 / WIRE_SCALE)

    live = jnp.repeat(jnp.repeat(touched_mask[0], TILE, axis=0), TILE, axis=1) > 0
    weight = params[0]
    first = moment_one[0]
    second = moment_two[0]
    first_new = 0.9 * first + 0.1 * grad
    second_new = 0.95 * second + 0.05 * grad * grad
    scaled_first = first_new * (1.0 / (1.0 - 0.9**10))
    scaled_second = second_new * (1.0 / (1.0 - 0.95**10))
    step = scaled_first / (jnp.sqrt(scaled_second) + 1e-08)
    weight_new = weight - 0.01 * (step + 0.1 * weight)
    out_weight = jnp.where(live, weight_new, weight)[None]
    out_first = jnp.where(live, first_new, first)[None]
    out_second = jnp.where(live, second_new, second)[None]
    return (out_weight, out_first, out_second)


def solution(mesh):
    rows = P(("dp", "expert", "opt"), None)
    state = P("expert", ("dp", "opt"), None)
    return jax.shard_map(
        per_device,
        mesh=mesh,
        in_specs=(rows, rows, P("dp", "expert", "opt", None, None), state, state, state, state),
        out_specs=(state, state, state),
        check_vma=False,
    )
```

```python
import functools

import jax
import jax.numpy as jnp
from jax import lax
from jax.experimental import pallas as pl
from jax.experimental.pallas import tpu as pltpu
from jax.sharding import PartitionSpec as P

TILE = 128
CAP = 32
EXPERTS = 16
N_DP = 8
HALF = 256
WIRE_SCALE = 16.0


def picks(routes, count):
    expert = lax.broadcasted_iota(jnp.int32, (EXPERTS, count), 0)
    named = routes[0:1, :] == expert
    for k in range(1, routes.shape[0]):
        named = jnp.logical_or(named, routes[k : k + 1, :] == expert)
    named = named.astype(jnp.float32)
    row = lax.broadcasted_iota(jnp.int32, (count, count), 0)
    column = lax.broadcasted_iota(jnp.int32, (count, count), 1)
    earlier = (row < column).astype(jnp.bfloat16)
    before = jnp.dot(named.astype(jnp.bfloat16), earlier, preferred_element_type=jnp.float32)
    slot_of = jnp.where(named > 0, before, -1.0).astype(jnp.int32)
    slot = lax.broadcasted_iota(jnp.int32, (CAP, count), 0)
    return jnp.concatenate(
        [(slot_of[e : e + 1, :] == slot).astype(jnp.float32) for e in range(EXPERTS)], axis=0
    ).astype(jnp.bfloat16)


def columns_of(r, core, pairs):
    starts = []
    for distance, other in pairs:
        up = 2 * lax.rem(r + distance, N_DP) + other
        down = 2 * lax.rem(r + (N_DP - distance), N_DP) + 1 - other
        block = jnp.where(core == 0, up, down)
        starts.append(pl.multiple_of(block * HALF, HALF))
    return starts


def dispatch_kernel(routes_ref, tokens_ref, out_ref, tokens_in, pick_ref, made, in_sems, out_sems, *, pairs):
    starts = columns_of(lax.axis_index("dp"), 0, pairs) + columns_of(lax.axis_index("dp"), 1, pairs)
    reads = [
        pltpu.make_async_copy(
            tokens_ref.at[:, pl.ds(start, HALF)],
            tokens_in.at[n // len(pairs), :, pl.ds(n % len(pairs) * HALF, HALF)],
            in_sems.at[n],
        )
        for n, start in enumerate(starts)
    ]
    for read in reads:
        read.start()
    pick_ref[...] = picks(routes_ref[...], tokens_ref.shape[0])
    rows = EXPERTS * CAP
    writes = []
    for core in range(2):
        for read in reads[core * len(pairs) : (core + 1) * len(pairs)]:
            read.wait()
        made[core] = jnp.dot(
            pick_ref[...], tokens_in[core], preferred_element_type=jnp.float32
        ).astype(made.dtype)
        write = pltpu.make_async_copy(
            made.at[core], out_ref.at[pl.ds(core * rows, rows), :], out_sems.at[core]
        )
        write.start()
        writes.append(write)
    for write in writes:
        write.wait()


def dispatch(routes, tokens, pairs, limit):
    rows = EXPERTS * CAP
    count = tokens.shape[0]
    blocks = 2 * len(pairs)
    hbm = pl.BlockSpec(memory_space=pltpu.HBM)
    return pl.pallas_call(
        functools.partial(dispatch_kernel, pairs=pairs),
        in_specs=[pl.BlockSpec(memory_space=pltpu.VMEM), hbm],
        out_specs=hbm,
        scratch_shapes=[
            pltpu.VMEM((2, count, len(pairs) * HALF), jnp.bfloat16),
            pltpu.VMEM((rows, count), jnp.bfloat16),
            pltpu.VMEM((2, rows, len(pairs) * HALF), jnp.bfloat16),
            pltpu.SemaphoreType.DMA((blocks,)),
            pltpu.SemaphoreType.DMA((2,)),
        ],
        out_shape=jax.ShapeDtypeStruct((2 * rows, len(pairs) * HALF), jnp.bfloat16),
        compiler_params=pltpu.CompilerParams(vmem_limit_bytes=limit),
        cost_estimate=pl.CostEstimate(
            flops=2 * rows * blocks * HALF * count,
            bytes_accessed=blocks * HALF * (count + rows) * 2,
            transcendentals=0,
        ),
        name="dispatch",
    )(routes, tokens)


def hold_kernel(x_ref, out_ref):
    out_ref[...] = x_ref[...]


def hold(x):
    vmem = pl.BlockSpec(memory_space=pltpu.VMEM)
    return pl.pallas_call(
        hold_kernel,
        in_specs=[vmem],
        out_specs=vmem,
        out_shape=jax.ShapeDtypeStruct(x.shape, x.dtype),
        compiler_params=pltpu.CompilerParams(vmem_limit_bytes=8 << 20),
        name="hold",
    )(x)


def product_kernel(arrived_ref, g_mine, g_other, out_ref, x_mine, x_other, sems, *, first):
    core = lax.axis_index("opt")
    columns = pl.ds(first * HALF, x_mine.shape[1])
    copies = [
        pltpu.make_async_copy(arrived_ref.at[core, :, columns], x_mine, sems.at[0]),
        pltpu.make_async_copy(arrived_ref.at[1 - core, :, columns], x_other, sems.at[1]),
    ]
    for copy in copies:
        copy.start()
    for copy in copies:
        copy.wait()

    def part(x, g):
        contract = (((0,), (0,)), ((), ()))
        p = lax.dot_general(x, g, contract, preferred_element_type=jnp.float32)
        return p.astype(jnp.bfloat16).astype(jnp.float32)

    tile = 768
    for n in range(0, out_ref.shape[1], tile):
        out_ref[:, n : n + tile] = WIRE_SCALE * (
            part(x_mine[...], g_mine[:, n : n + tile])
            + part(x_other[...], g_other[:, n : n + tile])
        )


def product(arrived, mine, other, first, count):
    slots, hidden = mine.shape
    rows = count * HALF
    vmem = pl.BlockSpec(memory_space=pltpu.VMEM)
    return pl.pallas_call(
        functools.partial(product_kernel, first=first),
        in_specs=[pl.BlockSpec(memory_space=pltpu.HBM), vmem, vmem],
        out_specs=vmem,
        scratch_shapes=[
            pltpu.VMEM((slots, rows), jnp.bfloat16),
            pltpu.VMEM((slots, rows), jnp.bfloat16),
            pltpu.SemaphoreType.DMA((2,)),
        ],
        out_shape=jax.ShapeDtypeStruct((rows, hidden), jnp.float32),
        compiler_params=pltpu.CompilerParams(vmem_limit_bytes=24 << 20),
        cost_estimate=pl.CostEstimate(
            flops=2 * 2 * slots * rows * hidden,
            bytes_accessed=4 * slots * (rows + hidden) + 4 * rows * hidden,
            transcendentals=0,
        ),
        name="product",
    )(arrived, mine, other)


def update_kernel(mask_ref, params, moment_one, moment_two, base, near, *refs, start):
    out_params, out_one, out_two = refs[-3:]
    rows, width = out_params.shape
    t = pl.program_id(0)
    for i in range(0, rows, TILE):
        for j in range(0, width, TILE):
            at = (pl.ds(i, TILE), pl.ds(pl.multiple_of(start + t * width + j, TILE), TILE))
            here = (pl.ds(i, TILE), pl.ds(pl.multiple_of(t * width + j, TILE), TILE))
            to = (pl.ds(i, TILE), pl.ds(j, TILE))
            live = mask_ref[i // TILE, (start + t * width + j) // TILE] > 0
            grad = (base[at] + near[here]) * (1.0 / WIRE_SCALE)
            weight, first, second = params[at], moment_one[at], moment_two[at]
            first_new = 0.9 * first + 0.1 * grad
            second_new = 0.95 * second + 0.05 * grad * grad
            scaled_first = first_new * (1.0 / (1.0 - 0.9**10))
            scaled_second = second_new * (1.0 / (1.0 - 0.95**10))
            step = scaled_first / (jnp.sqrt(scaled_second) + 1e-08)
            weight_new = weight - 0.01 * (step + 0.1 * weight)
            out_params[to] = jnp.where(live, weight_new, weight)
            out_one[to] = jnp.where(live, first_new, first)
            out_two[to] = jnp.where(live, second_new, second)


def update(mask, state, base, near, start, before):
    shape = base.shape
    width = 384
    done = start // width
    vmem = pl.BlockSpec(memory_space=pltpu.VMEM)
    return pl.pallas_call(
        functools.partial(update_kernel, start=start),
        grid=(near.shape[1] // width,),
        in_specs=[pl.BlockSpec(memory_space=pltpu.SMEM)]
        + [vmem] * 5
        + [pl.BlockSpec(memory_space=pl.ANY)] * len(before),
        out_specs=[pl.BlockSpec((shape[0], width), lambda t: (0, done + t))] * 3,
        out_shape=[jax.ShapeDtypeStruct(shape, jnp.float32)] * 3,
        input_output_aliases={6 + i: i for i in range(len(before))},
        compiler_params=pltpu.CompilerParams(vmem_limit_bytes=24 << 20),
        cost_estimate=pl.CostEstimate(
            flops=20 * near.size, bytes_accessed=28 * near.size, transcendentals=2 * near.size
        ),
        name="update",
    )(mask, *state, base, near, *before)


def after(x, *others):
    return lax.optimization_barrier((x,) + others)[0]


def per_device(tokens, routing, grad_gate, touched_mask, params, moment_one, moment_two):
    slots = EXPERTS * CAP
    routes = routing.T
    mine = grad_gate[0, 0, 0]
    other = lax.ppermute(mine, "opt", [(0, 1), (1, 0)])
    mine = hold(mine)

    ahead = [(i * 2 + o, ((i + (1 - 2 * o)) % N_DP) * 2 + o) for i in range(N_DP) for o in range(2)]
    across = [(i * 2 + o, ((i + (1 - 2 * o)) % N_DP) * 2 + 1 - o) for i in range(N_DP) for o in range(2)]

    def gathered(*pairs, limit=12 << 20):
        return dispatch(routes, tokens, pairs, limit)

    def exchange(sent):
        sent = sent.reshape(2 * EXPERTS, CAP, -1)
        return lax.all_to_all(sent, ("opt", "expert"), 0, 0, tiled=True).reshape(2, slots, -1)

    def totals(arrived, first, count):
        out = product(arrived, mine, other, first, count)
        return [out[j * HALF : (j + 1) * HALF] for j in range(count)]

    def plus(x, received):
        return x + received.astype(jnp.float32)

    def pack(x):
        return x.astype(jnp.float16)

    def shift(x, pairs):
        return lax.ppermute(x, ("dp", "opt"), pairs)

    sent_1 = gathered((4, 0), (3, 1), (3, 0), (2, 1), limit=60 << 20)
    arrived = exchange(sent_1)
    sent_2 = after(gathered((2, 0), (1, 1), (1, 0)), sent_1)
    sent_3 = after(gathered((0, 0)), sent_2)
    arrived, sent_2, sent_3, mine, other = lax.optimization_barrier((arrived, sent_2, sent_3, mine, other))
    four_a, three_b = totals(arrived, 0, 2)
    near_out, far_out = pack(four_a), pack(three_b)
    near = shift(near_out, ahead)
    late = exchange(after(sent_2, near_out))
    far = shift(far_out, ahead)
    three_a, two_b = totals(after(arrived, far_out), 2, 2)
    near_out = pack(plus(three_a, after(near, far_out)))
    near = shift(near_out, ahead)
    far_out = pack(plus(two_b, after(far, near_out)))
    far = shift(far_out, ahead)
    two_a, one_b, one_a = totals(late, 0, 3)
    near_out = pack(plus(two_a, after(near, far_out)))
    near = shift(near_out, ahead)
    far_out = pack(plus(one_b, after(far, near_out)))
    far = shift(far_out, across)
    last = exchange(after(sent_3, far_out))
    half = near_out.shape[1] // 2
    near = after(near, far_out)
    out_1 = pack(plus(one_a[:, :half], near[:, :half]))
    near_1 = shift(out_1, ahead)
    out_2 = pack(plus(one_a[:, half:], after(near, out_1)[:, half:]))
    near_2 = shift(out_2, ahead)
    (own,) = totals(after(last, out_1, out_2), 0, 1)
    base = plus(own, far)

    state = (params[0], moment_one[0], moment_two[0])
    outs = update(touched_mask[0], state, base, near_1.astype(jnp.float32), 0, ())
    outs = update(touched_mask[0], state, base, near_2.astype(jnp.float32), half, outs)
    return tuple(out[None] for out in outs)


def solution(mesh):
    rows = P(("dp", "expert", "opt"), None)
    state = P("expert", ("dp", "opt"), None)
    return jax.shard_map(
        per_device,
        mesh=mesh,
        in_specs=(rows, rows, P("dp", "expert", "opt", None, None), state, state, state, state),
        out_specs=(state, state, state),
        check_vma=False,
    )
```

```python
import functools

import jax
import jax.numpy as jnp
from jax import lax
from jax.experimental import pallas as pl
from jax.experimental.pallas import tpu as pltpu
from jax.sharding import PartitionSpec as P

TILE = 128
CAP = 32
EXPERTS = 16
N_DP = 8
HALF = 256
WIRE_SCALE = 16.0


def picks(routes, count):
    expert = lax.broadcasted_iota(jnp.int32, (EXPERTS, count), 0)
    named = routes[0:1, :] == expert
    for k in range(1, routes.shape[0]):
        named = jnp.logical_or(named, routes[k : k + 1, :] == expert)
    named = named.astype(jnp.float32)
    row = lax.broadcasted_iota(jnp.int32, (count, count), 0)
    column = lax.broadcasted_iota(jnp.int32, (count, count), 1)
    earlier = (row < column).astype(jnp.bfloat16)
    before = jnp.dot(named.astype(jnp.bfloat16), earlier, preferred_element_type=jnp.float32)
    slot_of = jnp.where(named > 0, before, -1.0).astype(jnp.int32)
    slot = lax.broadcasted_iota(jnp.int32, (CAP, count), 0)
    return jnp.concatenate(
        [(slot_of[e : e + 1, :] == slot).astype(jnp.float32) for e in range(EXPERTS)], axis=0
    ).astype(jnp.bfloat16)


def columns_of(r, core, blocks):
    starts = []
    for distance, other, offset, _ in blocks:
        up = 2 * lax.rem(r + distance, N_DP) + other
        down = 2 * lax.rem(r + (N_DP - distance), N_DP) + 1 - other
        starts.append(pl.multiple_of(jnp.where(core == 0, up, down) * HALF + offset, 128))
    return starts


def dispatch_kernel(routes_ref, tokens_ref, out_ref, tokens_in, pick_ref, made, in_sems, out_sems, *, blocks):
    r = lax.axis_index("dp")
    reads = []
    for core in range(2):
        place = 0
        for (*_, width), start in zip(blocks, columns_of(r, core, blocks)):
            read = pltpu.make_async_copy(
                tokens_ref.at[:, pl.ds(start, width)],
                tokens_in.at[core, :, pl.ds(place, width)],
                in_sems.at[len(reads)],
            )
            read.start()
            reads.append(read)
            place = place + width
    pick_ref[...] = picks(routes_ref[...], tokens_ref.shape[0])
    rows = EXPERTS * CAP
    writes = []
    for core in range(2):
        for read in reads[core * len(blocks) : (core + 1) * len(blocks)]:
            read.wait()
        made[core] = jnp.dot(
            pick_ref[...], tokens_in[core], preferred_element_type=jnp.float32
        ).astype(made.dtype)
        write = pltpu.make_async_copy(
            made.at[core], out_ref.at[pl.ds(core * rows, rows), :], out_sems.at[core]
        )
        write.start()
        writes.append(write)
    for write in writes:
        write.wait()


def dispatch(routes, tokens, blocks, limit):
    rows = EXPERTS * CAP
    count = tokens.shape[0]
    total = sum(width for *_, width in blocks)
    hbm = pl.BlockSpec(memory_space=pltpu.HBM)
    return pl.pallas_call(
        functools.partial(dispatch_kernel, blocks=blocks),
        in_specs=[pl.BlockSpec(memory_space=pltpu.VMEM), hbm],
        out_specs=hbm,
        scratch_shapes=[
            pltpu.VMEM((2, count, total), jnp.bfloat16),
            pltpu.VMEM((rows, count), jnp.bfloat16),
            pltpu.VMEM((2, rows, total), jnp.bfloat16),
            pltpu.SemaphoreType.DMA((2 * len(blocks),)),
            pltpu.SemaphoreType.DMA((2,)),
        ],
        out_shape=jax.ShapeDtypeStruct((2 * rows, total), jnp.bfloat16),
        compiler_params=pltpu.CompilerParams(vmem_limit_bytes=limit),
        cost_estimate=pl.CostEstimate(
            flops=4 * rows * total * count, bytes_accessed=4 * total * (count + rows), transcendentals=0
        ),
        name="dispatch",
    )(routes, tokens)


def hold_kernel(x_ref, out_ref):
    out_ref[...] = x_ref[...]


def hold(x):
    vmem = pl.BlockSpec(memory_space=pltpu.VMEM)
    return pl.pallas_call(
        hold_kernel,
        in_specs=[vmem],
        out_specs=vmem,
        out_shape=jax.ShapeDtypeStruct(x.shape, x.dtype),
        compiler_params=pltpu.CompilerParams(vmem_limit_bytes=8 << 20),
        name="hold",
    )(x)


def product_kernel(arrived_ref, g_mine, g_other, out_ref, x_mine, x_other, sems, *, first):
    core = lax.axis_index("opt")
    columns = pl.ds(first, x_mine.shape[1])
    copies = [
        pltpu.make_async_copy(arrived_ref.at[core, :, columns], x_mine, sems.at[0]),
        pltpu.make_async_copy(arrived_ref.at[1 - core, :, columns], x_other, sems.at[1]),
    ]
    for copy in copies:
        copy.start()
    for copy in copies:
        copy.wait()

    def part(x, g):
        contract = (((0,), (0,)), ((), ()))
        p = lax.dot_general(x, g, contract, preferred_element_type=jnp.float32)
        return p.astype(jnp.bfloat16).astype(jnp.float32)

    tile = 768
    for n in range(0, out_ref.shape[1], tile):
        out_ref[:, n : n + tile] = WIRE_SCALE * (
            part(x_mine[...], g_mine[:, n : n + tile])
            + part(x_other[...], g_other[:, n : n + tile])
        )


def product(arrived, mine, other, first, rows):
    slots, hidden = mine.shape
    vmem = pl.BlockSpec(memory_space=pltpu.VMEM)
    return pl.pallas_call(
        functools.partial(product_kernel, first=first),
        in_specs=[pl.BlockSpec(memory_space=pltpu.HBM), vmem, vmem],
        out_specs=vmem,
        scratch_shapes=[
            pltpu.VMEM((slots, rows), jnp.bfloat16),
            pltpu.VMEM((slots, rows), jnp.bfloat16),
            pltpu.SemaphoreType.DMA((2,)),
        ],
        out_shape=jax.ShapeDtypeStruct((rows, hidden), jnp.float32),
        compiler_params=pltpu.CompilerParams(vmem_limit_bytes=24 << 20),
        cost_estimate=pl.CostEstimate(
            flops=2 * 2 * slots * rows * hidden,
            bytes_accessed=4 * slots * (rows + hidden) + 4 * rows * hidden,
            transcendentals=0,
        ),
        name="product",
    )(arrived, mine, other)


def update_kernel(mask_ref, params, moment_one, moment_two, base, near, *refs, start):
    out_params, out_one, out_two = refs[-3:]
    rows, width = out_params.shape
    t = pl.program_id(0)
    for i in range(0, rows, TILE):
        for j in range(0, width, TILE):
            at = (pl.ds(i, TILE), pl.ds(pl.multiple_of(start + t * width + j, TILE), TILE))
            here = (pl.ds(i, TILE), pl.ds(pl.multiple_of(t * width + j, TILE), TILE))
            to = (pl.ds(i, TILE), pl.ds(j, TILE))
            live = mask_ref[i // TILE, (start + t * width + j) // TILE] > 0
            grad = (base[at] + near[here]) * (1.0 / WIRE_SCALE)
            weight, first, second = params[at], moment_one[at], moment_two[at]
            first_new = 0.9 * first + 0.1 * grad
            second_new = 0.95 * second + 0.05 * grad * grad
            scaled_first = first_new * (1.0 / (1.0 - 0.9**10))
            scaled_second = second_new * (1.0 / (1.0 - 0.95**10))
            step = scaled_first / (jnp.sqrt(scaled_second) + 1e-08)
            weight_new = weight - 0.01 * (step + 0.1 * weight)
            out_params[to] = jnp.where(live, weight_new, weight)
            out_one[to] = jnp.where(live, first_new, first)
            out_two[to] = jnp.where(live, second_new, second)


def update(mask, state, base, near, start, before):
    shape = base.shape
    width = 384
    done = start // width
    vmem = pl.BlockSpec(memory_space=pltpu.VMEM)
    return pl.pallas_call(
        functools.partial(update_kernel, start=start),
        grid=(near.shape[1] // width,),
        in_specs=[pl.BlockSpec(memory_space=pltpu.SMEM)]
        + [vmem] * 5
        + [pl.BlockSpec(memory_space=pl.ANY)] * len(before),
        out_specs=[pl.BlockSpec((shape[0], width), lambda t: (0, done + t))] * 3,
        out_shape=[jax.ShapeDtypeStruct(shape, jnp.float32)] * 3,
        input_output_aliases={6 + i: i for i in range(len(before))},
        compiler_params=pltpu.CompilerParams(vmem_limit_bytes=24 << 20),
        cost_estimate=pl.CostEstimate(
            flops=20 * near.size, bytes_accessed=28 * near.size, transcendentals=2 * near.size
        ),
        name="update",
    )(mask, *state, base, near, *before)


def after(x, *others):
    return lax.optimization_barrier((x,) + others)[0]


def per_device(tokens, routing, grad_gate, touched_mask, params, moment_one, moment_two):
    slots = EXPERTS * CAP
    routes = routing.T
    mine = grad_gate[0, 0, 0]
    other = lax.ppermute(mine, "opt", [(0, 1), (1, 0)])
    mine = hold(mine)

    ahead = [(i * 2 + o, ((i + (1 - 2 * o)) % N_DP) * 2 + o) for i in range(N_DP) for o in range(2)]
    across = [(i * 2 + o, ((i + (1 - 2 * o)) % N_DP) * 2 + 1 - o) for i in range(N_DP) for o in range(2)]

    def gathered(*blocks, limit=12 << 20):
        return dispatch(routes, tokens, blocks, limit)

    def exchange(sent):
        sent = sent.reshape(2 * EXPERTS, CAP, -1)
        return lax.all_to_all(sent, ("opt", "expert"), 0, 0, tiled=True).reshape(2, slots, -1)

    def totals(arrived, first, *widths):
        out = product(arrived, mine, other, first, sum(widths))
        return jnp.split(out, [sum(widths[:j]) for j in range(1, len(widths))]) if len(widths) > 1 else [out]

    def plus(x, received):
        return x + received.astype(jnp.float32)

    def pack(x):
        return x.astype(jnp.float16)

    def shift(x, pairs):
        return lax.ppermute(x, ("dp", "opt"), pairs)

    some = HALF // 2
    sent_1 = gathered((4, 0, 0, HALF), (3, 1, 0, HALF), (3, 0, 0, some), limit=60 << 20)
    arrived = exchange(sent_1)
    sent_2 = after(gathered((3, 0, some, some), (2, 1, 0, HALF), (2, 0, 0, HALF), (1, 1, 0, HALF)), sent_1)
    sent_3 = after(gathered((1, 0, 0, HALF), (0, 0, 0, HALF)), sent_2)
    arrived, sent_2, sent_3, mine, other = lax.optimization_barrier((arrived, sent_2, sent_3, mine, other))
    late = exchange(sent_2)
    four_a, three_b = totals(arrived, 0, HALF, HALF)
    near_out, far_out = pack(four_a), pack(three_b)
    near = shift(near_out, ahead)
    far = shift(far_out, ahead)
    (three_a,) = totals(after(arrived, far_out), 2 * HALF, some)
    near = after(near, three_a)
    near_out = pack(plus(three_a, near[:some]))
    near_1 = shift(near_out, ahead)
    three_a, two_b = totals(after(late, near_out), 0, some, HALF)
    near_out = pack(plus(three_a, near[some:]))
    near_2 = shift(near_out, ahead)
    far_out = pack(plus(two_b, after(far, near_out)))
    far = shift(far_out, ahead)
    last = exchange(after(sent_3, far_out))
    two_a, one_b = totals(after(late, far_out), some + HALF, HALF, HALF)
    near = after(jnp.concatenate([near_1, near_2]), two_a)
    near_out = pack(plus(two_a, near))
    near = shift(near_out, ahead)
    far_out = pack(plus(one_b, after(far, near_out)))
    far = shift(far_out, across)
    one_a, own = totals(after(last, far_out), 0, HALF, HALF)
    half = near_out.shape[1] // 2
    near = after(near, far_out)
    out_1 = pack(plus(one_a[:, :half], near[:, :half]))
    near_1 = shift(out_1, ahead)
    out_2 = pack(plus(one_a[:, half:], after(near, out_1)[:, half:]))
    near_2 = shift(out_2, ahead)
    base = plus(own, far)

    state = (params[0], moment_one[0], moment_two[0])
    outs = update(touched_mask[0], state, base, near_1.astype(jnp.float32), 0, ())
    outs = update(touched_mask[0], state, base, near_2.astype(jnp.float32), half, outs)
    return tuple(out[None] for out in outs)


def solution(mesh):
    rows = P(("dp", "expert", "opt"), None)
    state = P("expert", ("dp", "opt"), None)
    return jax.shard_map(
        per_device,
        mesh=mesh,
        in_specs=(rows, rows, P("dp", "expert", "opt", None, None), state, state, state, state),
        out_specs=(state, state, state),
        check_vma=False,
    )
```

```python
import functools

import jax
import jax.numpy as jnp
from jax import lax
from jax.experimental import pallas as pl
from jax.experimental.pallas import tpu as pltpu
from jax.sharding import PartitionSpec as P

TILE = 128
CAP = 32
EXPERTS = 16
N_DP = 8
HALF = 256
WIRE_SCALE = 16.0


def picks(routes, count):
    expert = lax.broadcasted_iota(jnp.int32, (EXPERTS, count), 0)
    named = routes[0:1, :] == expert
    for k in range(1, routes.shape[0]):
        named = jnp.logical_or(named, routes[k : k + 1, :] == expert)
    named = named.astype(jnp.float32)
    row = lax.broadcasted_iota(jnp.int32, (count, count), 0)
    column = lax.broadcasted_iota(jnp.int32, (count, count), 1)
    earlier = (row < column).astype(jnp.bfloat16)
    before = jnp.dot(named.astype(jnp.bfloat16), earlier, preferred_element_type=jnp.float32)
    slot_of = jnp.where(named > 0, before, -1.0).astype(jnp.int32)
    slot = lax.broadcasted_iota(jnp.int32, (CAP, count), 0)
    return jnp.concatenate(
        [(slot_of[e : e + 1, :] == slot).astype(jnp.float32) for e in range(EXPERTS)], axis=0
    ).astype(jnp.bfloat16)


def columns_of(r, core, blocks):
    starts = []
    for distance, other, offset, _ in blocks:
        up = 2 * lax.rem(r + distance, N_DP) + other
        down = 2 * lax.rem(r + (N_DP - distance), N_DP) + 1 - other
        starts.append(pl.multiple_of(jnp.where(core == 0, up, down) * HALF + offset, 128))
    return starts


def dispatch_kernel(routes_ref, tokens_ref, out_ref, tokens_in, pick_ref, made, in_sems, out_sems, *, blocks):
    r = lax.axis_index("dp")
    reads = []
    for core in range(2):
        place = 0
        for (*_, width), start in zip(blocks, columns_of(r, core, blocks)):
            read = pltpu.make_async_copy(
                tokens_ref.at[:, pl.ds(start, width)],
                tokens_in.at[core, :, pl.ds(place, width)],
                in_sems.at[len(reads)],
            )
            read.start()
            reads.append(read)
            place = place + width
    pick_ref[...] = picks(routes_ref[...], tokens_ref.shape[0])
    rows = EXPERTS * CAP
    writes = []
    for core in range(2):
        for read in reads[core * len(blocks) : (core + 1) * len(blocks)]:
            read.wait()
        made[core] = jnp.dot(
            pick_ref[...], tokens_in[core], preferred_element_type=jnp.float32
        ).astype(made.dtype)
        write = pltpu.make_async_copy(
            made.at[core], out_ref.at[pl.ds(core * rows, rows), :], out_sems.at[core]
        )
        write.start()
        writes.append(write)
    for write in writes:
        write.wait()


def dispatch(routes, tokens, blocks, limit):
    rows = EXPERTS * CAP
    count = tokens.shape[0]
    total = sum(width for *_, width in blocks)
    hbm = pl.BlockSpec(memory_space=pltpu.HBM)
    return pl.pallas_call(
        functools.partial(dispatch_kernel, blocks=blocks),
        in_specs=[pl.BlockSpec(memory_space=pltpu.VMEM), hbm],
        out_specs=hbm,
        scratch_shapes=[
            pltpu.VMEM((2, count, total), jnp.bfloat16),
            pltpu.VMEM((rows, count), jnp.bfloat16),
            pltpu.VMEM((2, rows, total), jnp.bfloat16),
            pltpu.SemaphoreType.DMA((2 * len(blocks),)),
            pltpu.SemaphoreType.DMA((2,)),
        ],
        out_shape=jax.ShapeDtypeStruct((2 * rows, total), jnp.bfloat16),
        compiler_params=pltpu.CompilerParams(vmem_limit_bytes=limit),
        cost_estimate=pl.CostEstimate(
            flops=4 * rows * total * count, bytes_accessed=4 * total * (count + rows), transcendentals=0
        ),
        name="dispatch",
    )(routes, tokens)


def hold_kernel(x_ref, out_ref):
    out_ref[...] = x_ref[...]


def hold(x):
    vmem = pl.BlockSpec(memory_space=pltpu.VMEM)
    return pl.pallas_call(
        hold_kernel,
        in_specs=[vmem],
        out_specs=vmem,
        out_shape=jax.ShapeDtypeStruct(x.shape, x.dtype),
        compiler_params=pltpu.CompilerParams(vmem_limit_bytes=8 << 20),
        name="hold",
    )(x)


def product_kernel(arrived_ref, g_mine, g_other, out_ref, x_mine, x_other, sems, *, first):
    core = lax.axis_index("opt")
    columns = pl.ds(first, x_mine.shape[1])
    copies = [
        pltpu.make_async_copy(arrived_ref.at[core, :, columns], x_mine, sems.at[0]),
        pltpu.make_async_copy(arrived_ref.at[1 - core, :, columns], x_other, sems.at[1]),
    ]
    for copy in copies:
        copy.start()
    for copy in copies:
        copy.wait()

    def part(x, g):
        contract = (((0,), (0,)), ((), ()))
        p = lax.dot_general(x, g, contract, preferred_element_type=jnp.float32)
        return p.astype(jnp.bfloat16).astype(jnp.float32)

    tile = 768
    for n in range(0, out_ref.shape[1], tile):
        out_ref[:, n : n + tile] = WIRE_SCALE * (
            part(x_mine[...], g_mine[:, n : n + tile])
            + part(x_other[...], g_other[:, n : n + tile])
        )


def product(arrived, mine, other, first, rows):
    slots, hidden = mine.shape
    vmem = pl.BlockSpec(memory_space=pltpu.VMEM)
    return pl.pallas_call(
        functools.partial(product_kernel, first=first),
        in_specs=[pl.BlockSpec(memory_space=pltpu.HBM), vmem, vmem],
        out_specs=vmem,
        scratch_shapes=[
            pltpu.VMEM((slots, rows), jnp.bfloat16),
            pltpu.VMEM((slots, rows), jnp.bfloat16),
            pltpu.SemaphoreType.DMA((2,)),
        ],
        out_shape=jax.ShapeDtypeStruct((rows, hidden), jnp.float32),
        compiler_params=pltpu.CompilerParams(vmem_limit_bytes=24 << 20),
        cost_estimate=pl.CostEstimate(
            flops=2 * 2 * slots * rows * hidden,
            bytes_accessed=4 * slots * (rows + hidden) + 4 * rows * hidden,
            transcendentals=0,
        ),
        name="product",
    )(arrived, mine, other)


def update_kernel(mask_ref, params, moment_one, moment_two, base, near, *refs, start):
    out_params, out_one, out_two = refs[-3:]
    rows, width = out_params.shape
    t = pl.program_id(0)
    for i in range(0, rows, TILE):
        for j in range(0, width, TILE):
            at = (pl.ds(i, TILE), pl.ds(pl.multiple_of(start + t * width + j, TILE), TILE))
            here = (pl.ds(i, TILE), pl.ds(pl.multiple_of(t * width + j, TILE), TILE))
            to = (pl.ds(i, TILE), pl.ds(j, TILE))
            live = mask_ref[i // TILE, (start + t * width + j) // TILE] > 0
            grad = (base[at] + near[here]) * (1.0 / WIRE_SCALE)
            weight, first, second = params[at], moment_one[at], moment_two[at]
            first_new = 0.9 * first + 0.1 * grad
            second_new = 0.95 * second + 0.05 * grad * grad
            scaled_first = first_new * (1.0 / (1.0 - 0.9**10))
            scaled_second = second_new * (1.0 / (1.0 - 0.95**10))
            step = scaled_first / (jnp.sqrt(scaled_second) + 1e-08)
            weight_new = weight - 0.01 * (step + 0.1 * weight)
            out_params[to] = jnp.where(live, weight_new, weight)
            out_one[to] = jnp.where(live, first_new, first)
            out_two[to] = jnp.where(live, second_new, second)


def update(mask, state, base, near, start, before):
    shape = base.shape
    width = 384
    done = start // width
    vmem = pl.BlockSpec(memory_space=pltpu.VMEM)
    return pl.pallas_call(
        functools.partial(update_kernel, start=start),
        grid=(near.shape[1] // width,),
        in_specs=[pl.BlockSpec(memory_space=pltpu.SMEM)]
        + [vmem] * 5
        + [pl.BlockSpec(memory_space=pl.ANY)] * len(before),
        out_specs=[pl.BlockSpec((shape[0], width), lambda t: (0, done + t))] * 3,
        out_shape=[jax.ShapeDtypeStruct(shape, jnp.float32)] * 3,
        input_output_aliases={6 + i: i for i in range(len(before))},
        compiler_params=pltpu.CompilerParams(vmem_limit_bytes=24 << 20),
        cost_estimate=pl.CostEstimate(
            flops=20 * near.size, bytes_accessed=28 * near.size, transcendentals=2 * near.size
        ),
        name="update",
    )(mask, *state, base, near, *before)


def after(x, *others):
    return lax.optimization_barrier((x,) + others)[0]


def per_device(tokens, routing, grad_gate, touched_mask, params, moment_one, moment_two):
    slots = EXPERTS * CAP
    routes = routing.T
    mine = grad_gate[0, 0, 0]
    other = lax.ppermute(mine, "opt", [(0, 1), (1, 0)])
    mine = hold(mine)

    ahead = [(i * 2 + o, ((i + (1 - 2 * o)) % N_DP) * 2 + o) for i in range(N_DP) for o in range(2)]
    across = [(i * 2 + o, ((i + (1 - 2 * o)) % N_DP) * 2 + 1 - o) for i in range(N_DP) for o in range(2)]

    def gathered(*blocks, limit=12 << 20):
        return dispatch(routes, tokens, blocks, limit)

    def exchange(sent):
        sent = sent.reshape(2 * EXPERTS, CAP, -1)
        return lax.all_to_all(sent, ("opt", "expert"), 0, 0, tiled=True).reshape(2, slots, -1)

    def totals(arrived, first, *widths):
        out = product(arrived, mine, other, first, sum(widths))
        return jnp.split(out, [sum(widths[:j]) for j in range(1, len(widths))]) if len(widths) > 1 else [out]

    def plus(x, received):
        return x + received.astype(jnp.float32)

    def pack(x):
        return x.astype(jnp.float16)

    def shift(x, pairs):
        return lax.ppermute(x, ("dp", "opt"), pairs)

    some = HALF // 2
    sent_1 = gathered((4, 0, 0, HALF), (3, 1, 0, HALF), (3, 0, 0, some), limit=60 << 20)
    arrived = exchange(sent_1)
    sent_2 = after(gathered((3, 0, some, some), (2, 1, 0, HALF), (2, 0, 0, HALF), (1, 1, 0, HALF)), sent_1)
    sent_3 = after(gathered((1, 0, 0, HALF), (0, 0, 0, HALF)), sent_2)
    arrived, sent_2, sent_3, mine, other = lax.optimization_barrier((arrived, sent_2, sent_3, mine, other))
    late = exchange(sent_2)
    four_a, three_b = totals(arrived, 0, HALF, HALF)
    near_out, far_out = pack(four_a), pack(three_b)
    near = shift(near_out, ahead)
    far = shift(far_out, ahead)
    (three_a,) = totals(after(arrived, far_out), 2 * HALF, some)
    near = after(near, three_a)
    near_out = pack(plus(three_a, near[:some]))
    near_1 = shift(near_out, ahead)
    three_a, two_b = totals(after(late, near_out), 0, some, HALF)
    near_out = pack(plus(three_a, near[some:]))
    near_2 = shift(near_out, ahead)
    far_out = pack(plus(two_b, after(far, near_out)))
    far = shift(far_out, ahead)
    last = exchange(after(sent_3, far_out))
    (two_a,) = totals(after(late, far_out), some + HALF, HALF)
    near = after(jnp.concatenate([near_1, near_2]), two_a)
    near_out = pack(plus(two_a, near))
    near = shift(near_out, ahead)
    (one_b,) = totals(after(late, near_out), some + 2 * HALF, HALF)
    far_out = pack(plus(one_b, after(far, near_out)))
    far = shift(far_out, across)
    one_a, own = totals(after(last, far_out), 0, HALF, HALF)
    half = near_out.shape[1] // 2
    near = after(near, far_out)
    out_1 = pack(plus(one_a[:, :half], near[:, :half]))
    near_1 = shift(out_1, ahead)
    out_2 = pack(plus(one_a[:, half:], after(near, out_1)[:, half:]))
    near_2 = shift(out_2, ahead)
    base = plus(own, far)

    state = (params[0], moment_one[0], moment_two[0])
    outs = update(touched_mask[0], state, base, near_1.astype(jnp.float32), 0, ())
    outs = update(touched_mask[0], state, base, near_2.astype(jnp.float32), half, outs)
    return tuple(out[None] for out in outs)


def solution(mesh):
    rows = P(("dp", "expert", "opt"), None)
    state = P("expert", ("dp", "opt"), None)
    return jax.shard_map(
        per_device,
        mesh=mesh,
        in_specs=(rows, rows, P("dp", "expert", "opt", None, None), state, state, state, state),
        out_specs=(state, state, state),
        check_vma=False,
    )
```
